256 devices in a mesh: ctx: 32 (over y_lo, z, core), tp: 8 (over x, y_hi).
Axes of the slice: x: 4, y: 4 (y_hi: 2, y_lo: 2; y = y_hi * 2 + y_lo), z: 8, core: 2. Of those that a mesh axis runs over, the one named last changes fastest.
Arguments:
- queries: bfloat16 [4096, 8192], P('ctx', 'tp'), may hold values from -6 to 6
- keys_values: bfloat16 [4096, 1024], P('ctx', 'tp'), may hold values from -6 to 6
- forward_out: bfloat16 [4096, 8192], P('ctx', 'tp'), may hold values from -6 to 6
- out_grad: bfloat16 [4096, 8192], P('ctx', 'tp'), may hold values from -6 to 6
- kv_weight: bfloat16 [14848, 1024], P(None, 'tp'), may hold values from -3 to 3
- span_table: int32 [64], replicated, may hold values from 0 to 63, each once
Outputs:
- query_grad: bfloat16 [4096, 8192], P('ctx', 'tp')
- input_grad: bfloat16 [4096, 14848], P('ctx', 'tp')
The draws below stay inside these ranges and needn't reach their ends.
Inputs may be any that keep to these rules, and one draw needn't show every extreme that they name: `span_table`: a permutation: every sequence block appears once.
All inputs are finite; a program needn't handle non-finite values.
Results may differ from the reference program's by a relative error of at most 0.0057.
Values may be sent and summed in bfloat16 or wider, within the bound.
No kernel may reach another device: no remote copies, remote signals or barrier semaphores. Data moves between devices by JAX's collectives and lax.ppermute only.
A program may use at most 64 MiB of HBM per device.

```python
import jax
import jax.numpy as jnp
from jax import lax

D = 14848
HEAD = 64
HG = 16
KV = 8
HEADS = 128
SEQ = 4096
SPAN = 64
SPANS = 64
KBLOCK = 512


def draw_queries(key, part):
    key = jax.random.fold_in(key, 1)
    return jnp.clip(jax.random.normal(key, (SEQ, HEADS * HEAD)), -4.0, 4.0).astype(jnp.bfloat16)


def draw_keys_values(key, part):
    key = jax.random.fold_in(key, 3)
    return jnp.clip(jax.random.normal(key, (SEQ, KV * 2 * HEAD)), -4.0, 4.0).astype(jnp.bfloat16)


def steps_of(rng, dims, cuts, low, top_value):
    def one(dim, parts):
        heights = jax.random.uniform(jax.random.fold_in(jax.random.fold_in(rng, 6), dim), (parts,), jnp.float32, low / len(cuts), top_value / len(cuts))
        return jnp.repeat(jnp.exp(heights), dims[dim] // parts).reshape((-1,) + (1,) * (len(dims) - dim - 1))

    loudness = one(*cuts[0])
    for cut in cuts[1:]:
        loudness = loudness * one(*cut)
    return loudness


def bell_draw(stream_key, shape, deviation, reach, pieces=(), kind=jnp.bfloat16):
    loudness = steps_of(stream_key, shape, pieces, -0.22, 0.18) if pieces else 1.0
    drawn = jax.random.normal(stream_key, shape, jnp.float32) * deviation * loudness
    return jnp.minimum(jnp.maximum(drawn, -reach), reach).astype(kind)


def setup_inputs(seed: int = 0) -> dict:
    key_of = jax.random.split(jax.random.key(seed), 7)
    return {
        "queries": draw_queries(jax.random.fold_in(key_of[6], 71), 0),
        "keys_values": draw_keys_values(jax.random.fold_in(key_of[6], 71), 0),
        "forward_out": bell_draw(key_of[2], (SEQ, HEADS * HEAD), 1.0, 6.0, ((0, 32), (1, 8))),
        "out_grad": bell_draw(key_of[3], (SEQ, HEADS * HEAD), 1.0, 6.0, ((0, 32), (1, 8))),
        "kv_weight": bell_draw(key_of[4], (D, KV * 2 * HEAD), 0.5, 3.0, ((1, 8),)),
        "span_table": jax.random.permutation(key_of[5], SPANS).astype(jnp.int32),
    }


softmax_scale = 0.125
masked_score = -1.0e30


def reference(queries, keys_values, forward_out, out_grad, kv_weight, span_table):
    row_ids = jnp.arange(SEQ, dtype=jnp.int32)
    position = (span_table[row_ids // SPAN] * SPAN + row_ids % SPAN).astype(jnp.int32)
    query_parts = []
    kv_parts = []
    for group_index in range(KV):
        low = group_index * HG * HEAD
        query_cols = queries[:, low:low + HG * HEAD].reshape(SEQ, HG, HEAD).astype(jnp.float32)
        grad_cols = out_grad[:, low:low + HG * HEAD].reshape(SEQ, HG, HEAD).astype(jnp.float32)
        forward_cols = forward_out[:, low:low + HG * HEAD].reshape(SEQ, HG, HEAD).astype(jnp.float32)
        key_low = group_index * 2 * HEAD
        key_cols = keys_values[:, key_low:key_low + HEAD].astype(jnp.float32)
        value_cols = keys_values[:, key_low + HEAD:key_low + 2 * HEAD].astype(jnp.float32)
        grad_dot = jnp.sum(grad_cols * forward_cols, axis=2)

        def one_block(running, block_index):
            key_sum, value_sum = running
            first_row = (block_index * KBLOCK).astype(jnp.int32)
            query_block = lax.dynamic_slice_in_dim(query_cols, first_row, KBLOCK, 0)
            grad_block = lax.dynamic_slice_in_dim(grad_cols, first_row, KBLOCK, 0)
            dot_block = lax.dynamic_slice_in_dim(grad_dot, first_row, KBLOCK, 0)
            query_pos = lax.dynamic_slice_in_dim(position, first_row, KBLOCK, 0)
            visible = (position[None, :] <= query_pos[:, None])[None]
            scores = jnp.einsum("qhd,kd->hqk", query_block, key_cols) * softmax_scale
            scores = jnp.where(visible, scores, masked_score)
            row_top = jnp.max(scores, axis=2)
            row_total = jnp.sum(jnp.where(visible, jnp.exp(scores - row_top[:, :, None]), 0.0), axis=2)
            lse = row_top + jnp.log(row_total)
            probs = jnp.where(visible, jnp.exp(scores - lse[:, :, None]), 0.0)
            weights = probs.astype(jnp.bfloat16).astype(jnp.float32)
            dprobs = jnp.einsum("qhd,kd->hqk", grad_block, value_cols)
            dscores = (probs * (dprobs - dot_block.T[:, :, None])).astype(jnp.bfloat16).astype(jnp.float32)
            query_grad = (jnp.einsum("hqk,kd->qhd", dscores, key_cols) * softmax_scale).astype(jnp.bfloat16)
            key_sum = key_sum + jnp.einsum("hqk,qhd->kd", dscores, query_block) * softmax_scale
            value_sum = value_sum + jnp.einsum("hqk,qhd->kd", weights, grad_block)
            return (key_sum, value_sum), query_grad

        start = (jnp.zeros((SEQ, HEAD), jnp.float32), jnp.zeros((SEQ, HEAD), jnp.float32))
        (key_sum, value_sum), query_blocks = lax.scan(one_block, start, jnp.arange(SEQ // KBLOCK, dtype=jnp.int32))
        query_parts.append(query_blocks.reshape(SEQ, HG * HEAD))
        kv_parts.append(key_sum.astype(jnp.bfloat16))
        kv_parts.append(value_sum.astype(jnp.bfloat16))
    query_grad = jnp.concatenate(query_parts, axis=1)
    kv_grad = jnp.concatenate(kv_parts, axis=1)
    input_grad = lax.dot_general(kv_grad, kv_weight, (((1,), (1,)), ((), ())), preferred_element_type=jnp.float32)
    return query_grad, input_grad.astype(jnp.bfloat16)
```

```python
import functools

import jax
import jax.numpy as jnp
from jax import lax
from jax.experimental import pallas as pl
from jax.experimental.pallas import tpu as pltpu
from jax.sharding import PartitionSpec as P

HEAD = 64
SPAN = 64
BLOCK = 256
PAIR = 2 * HEAD
SCALE = 0.125
LOG2E = 1.4426950408889634
MASKED = -1e30

f32 = jnp.float32
bf16 = jnp.bfloat16


def dot_t(a, b):
    return lax.dot_general(a, b, (((1,), (1,)), ((), ())), preferred_element_type=f32)


def dot(a, b):
    return lax.dot_general(a, b, (((1,), (0,)), ((), ())), preferred_element_type=f32)


def swap_halves(x):
    return pltpu.roll(x.astype(f32), HEAD, 1)


def attention_kernel(
    slot_pos,
    my_pos,
    kv_a,
    kv_b,
    rows_a,
    rows_b,
    dq_a,
    dq_b,
    dkv_a,
    dkv_b,
    kv_sorted,
    kk,
    va,
    av,
    kt,
    scores,
    acc1,
    acc2,
    dqt,
):
    half_slots = kv_a.shape[0]
    blocks = kk.shape[0]
    per_block = BLOCK // SPAN
    width = dq_a.shape[1]
    pairs = width // PAIR
    qcount = pairs * SPAN

    def place(slot, _):
        for which, src in enumerate((kv_a, kv_b)):
            p = slot_pos[which * half_slots + slot]
            row = pl.multiple_of((p % per_block) * SPAN, SPAN)
            kv_sorted[p // per_block, pl.ds(row, SPAN), :] = src[slot]
        return 0

    lax.fori_loop(0, half_slots, place, 0)

    lane_k = lax.broadcasted_iota(jnp.int32, (BLOCK, PAIR), 1)
    low_k = lane_k < HEAD

    def prepare(b, _):
        kv = kv_sorted[b].astype(f32)
        vk = pltpu.roll(kv, HEAD, 1)
        kk[b] = jnp.where(low_k, kv, vk).astype(bf16)
        ones_hi = ((lane_k >= HEAD) & (lane_k < HEAD + 3)).astype(f32)
        ones_lo = (lane_k < 3).astype(f32)
        va[b] = jnp.where(low_k, vk, ones_hi).astype(bf16)
        av[b] = jnp.where(low_k, ones_lo, kv).astype(bf16)
        kt[b] = jnp.transpose(kv)[:HEAD].astype(bf16)
        acc1[b] = jnp.zeros((BLOCK, PAIR), f32)
        acc2[b] = jnp.zeros((BLOCK, PAIR), f32)
        return 0

    lax.fori_loop(0, blocks, prepare, 0)

    lane_q = lax.broadcasted_iota(jnp.int32, (qcount, PAIR), 1)
    low_q = lane_q < HEAD
    key_row = lax.broadcasted_iota(jnp.int32, (BLOCK, qcount), 0)
    query_row = lax.broadcasted_iota(jnp.int32, (BLOCK, qcount), 1) % SPAN

    def one_span(pos, rows, row, dq_out):
        def stacked(part):
            return jnp.concatenate(
                [
                    rows[pl.ds(row, SPAN), part * width + p * PAIR : part * width + (p + 1) * PAIR]
                    for p in range(pairs)
                ],
                axis=0,
            )

        q = stacked(0)
        do = stacked(1)
        fo = stacked(2)
        qf = q.astype(f32)
        dof = do.astype(f32)
        q2 = qf * (SCALE * LOG2E)
        hi = q2.astype(bf16).astype(f32)
        lo_rolled = pltpu.roll(q2 - hi, HEAD, 1)
        q_e = jnp.where(low_q, hi, lo_rolled).astype(bf16)
        q_o = jnp.where(low_q, lo_rolled, hi).astype(bf16)
        prod = dof * fo.astype(f32)

        def parts(d):
            d = -d
            a = d.astype(bf16).astype(f32)
            b = (d - a).astype(bf16).astype(f32)
            return a, b, d - a - b

        def with_parts(d, base, keep):
            a, b, c = parts(d)
            at = 0 if keep else HEAD
            aux = jnp.where(lane_q == at, a, jnp.where(lane_q == at + 1, b, jnp.where(lane_q == at + 2, c, 0.0)))
            return jnp.where(low_q != keep, base, aux).astype(bf16)

        d_e = jnp.sum(jnp.where(low_q, prod, 0.0), axis=1, keepdims=True)
        d_o = jnp.sum(jnp.where(low_q, 0.0, prod), axis=1, keepdims=True)
        do_e = with_parts(d_e, dof, False)
        do_o = with_parts(d_o, dof, True)
        zero = jnp.zeros_like(qf)
        qe0 = jnp.where(low_q, qf, zero).astype(bf16)
        q0o = jnp.where(low_q, zero, qf).astype(bf16)
        doe0 = jnp.where(low_q, dof, zero).astype(bf16)
        do0o = jnp.where(low_q, zero, dof).astype(bf16)

        last = pos // per_block

        def stats(b, running, masked):
            new = []
            for e, qq in enumerate((q_e, q_o)):
                m, l = running[e]
                s = dot_t(kk[b], qq)
                if masked:
                    s = jnp.where(key_row <= (pos % per_block) * SPAN + query_row, s, MASKED)
                scores[b, :, e * qcount : (e + 1) * qcount] = s
                top = jnp.maximum(m, jnp.max(s, axis=0, keepdims=True))
                l = l * jnp.exp2(m - top) + jnp.sum(jnp.exp2(s - top), axis=0, keepdims=True)
                new.append((top, l))
            return tuple(new)

        init = (jnp.full((1, qcount), MASKED, f32), jnp.zeros((1, qcount), f32))
        running = lax.fori_loop(0, last, functools.partial(stats, masked=False), (init, init))
        running = stats(last, running, True)
        lse = [m + jnp.log2(l) for m, l in running]

        dqt[...] = jnp.zeros_like(dqt)

        def grads(b, _):
            ps, dss = [], []
            for e, (v, dd) in enumerate(((va, do_e), (av, do_o))):
                p = jnp.exp2(scores[b, :, e * qcount : (e + 1) * qcount] - lse[e])
                dp = dot_t(v[b], dd)
                ps.append(p.astype(bf16))
                dss.append((p * dp).astype(bf16))
            acc1[b] += dot(dss[0], qe0) + dot(ps[1], do0o)
            acc2[b] += dot(dss[1], q0o) + dot(ps[0], doe0)
            dqt[0:HEAD] += dot(kt[b], dss[0])
            dqt[HEAD:PAIR] += dot(kt[b], dss[1])
            return 0

        lax.fori_loop(0, last + 1, grads, 0)
        dq = (jnp.transpose(dqt[...]) * SCALE).astype(bf16)
        for p in range(pairs):
            dq_out[pl.ds(row, SPAN), p * PAIR : (p + 1) * PAIR] = dq[p * SPAN : (p + 1) * SPAN]

    for which, (rows, dq_out) in enumerate(((rows_a, dq_a), (rows_b, dq_b))):
        spans = rows.shape[0] // SPAN

        def step(i, _):
            one_span(my_pos[which * spans + i], rows, pl.multiple_of(i * SPAN, SPAN), dq_out)
            return 0

        lax.fori_loop(0, spans, step, 0)

    lane_s = lax.broadcasted_iota(jnp.int32, (SPAN, PAIR), 1)
    factor = jnp.where(lane_s < HEAD, SCALE, 1.0)

    def collect(slot, _):
        for which, dst in enumerate((dkv_a, dkv_b)):
            p = slot_pos[which * half_slots + slot]
            row = pl.multiple_of((p % per_block) * SPAN, SPAN)
            a1 = acc1[p // per_block, pl.ds(row, SPAN), :]
            a2 = acc2[p // per_block, pl.ds(row, SPAN), :]
            dst[slot] = ((a1 + pltpu.roll(a2, HEAD, 1)) * factor).astype(bf16)
        return 0

    lax.fori_loop(0, half_slots, collect, 0)


def attention_grads(slot_pos, my_pos, kv_a, kv_b, rows_a, rows_b):
    slots = 2 * kv_a.shape[0]
    blocks = slots * SPAN // BLOCK
    width = rows_a.shape[1] // 3
    qcount = width // PAIR * SPAN
    smem = pl.BlockSpec(memory_space=pltpu.SMEM)
    vmem = pl.BlockSpec(memory_space=pltpu.VMEM)
    tokens = rows_a.shape[0]
    pairs_of = slots * SPAN * tokens * 2 * width // HEAD
    return pl.pallas_call(
        attention_kernel,
        out_shape=(
            jax.ShapeDtypeStruct((tokens, width), bf16),
            jax.ShapeDtypeStruct((tokens, width), bf16),
            jax.ShapeDtypeStruct(kv_a.shape, bf16),
            jax.ShapeDtypeStruct(kv_b.shape, bf16),
        ),
        in_specs=[smem, smem, vmem, vmem, vmem, vmem],
        out_specs=(vmem, vmem, vmem, vmem),
        scratch_shapes=[
            pltpu.VMEM((blocks, BLOCK, PAIR), bf16),
            pltpu.VMEM((blocks, BLOCK, PAIR), bf16),
            pltpu.VMEM((blocks, BLOCK, PAIR), bf16),
            pltpu.VMEM((blocks, BLOCK, PAIR), bf16),
            pltpu.VMEM((blocks, HEAD, BLOCK), bf16),
            pltpu.VMEM((blocks, BLOCK, 2 * qcount), f32),
            pltpu.VMEM((blocks, BLOCK, PAIR), f32),
            pltpu.VMEM((blocks, BLOCK, PAIR), f32),
            pltpu.VMEM((PAIR, qcount), f32),
        ],
        compiler_params=pltpu.CompilerParams(vmem_limit_bytes=48 * 1024 * 1024),
        cost_estimate=pl.CostEstimate(
            flops=pairs_of * HEAD * 2 * 5 * 4, bytes_accessed=6 << 20, transcendentals=pairs_of
        ),
    )(slot_pos, my_pos, kv_a, kv_b, rows_a, rows_b)


def project_kernel(kv_ref, w_ref, out_ref):
    total = dot_t(kv_ref[0], w_ref[0])
    for g in range(1, kv_ref.shape[0]):
        total = total + dot_t(kv_ref[g], w_ref[g])
    out_ref[...] = total.astype(bf16)


def project(kv, w):
    vmem = pl.BlockSpec(memory_space=pltpu.VMEM)
    return pl.pallas_call(
        project_kernel,
        out_shape=jax.ShapeDtypeStruct((kv.shape[1], w.shape[1]), bf16),
        in_specs=[vmem, vmem],
        out_specs=vmem,
        compiler_params=pltpu.CompilerParams(vmem_limit_bytes=32 * 1024 * 1024),
        cost_estimate=pl.CostEstimate(
            flops=2 * kv.size * w.shape[1], bytes_accessed=2 * w.size, transcendentals=0
        ),
    )(kv, w)


def on_device(queries, keys_values, forward_out, out_grad, kv_weight, span_table):
    tokens = queries.shape[0]
    half = queries.shape[1] // 2
    me = lax.axis_index("ctx")
    core = me % 2
    count = lax.axis_size("ctx")
    groups = lax.axis_size("tp")
    chips = count // 2
    same_core = [[2 * chip + k for chip in range(chips)] for k in range(2)]
    other_core = [(i, i ^ 1) for i in range(count)]

    def to_all(x, n):
        return jnp.broadcast_to(x[None], (n,) + x.shape)

    def exchanged(x):
        return lax.ppermute(x, "ctx", other_core)

    features = kv_weight.shape[0] // groups
    weight = lax.all_to_all(kv_weight.reshape(groups, features, kv_weight.shape[1]), "tp", 0, 0)

    kv_a = lax.all_to_all(to_all(keys_values, chips), "ctx", 0, 0, axis_index_groups=same_core)
    kv_b = exchanged(kv_a)

    def my_heads(k):
        return [lax.dynamic_slice_in_dim(x, k * half, half, 1) for x in (queries, out_grad, forward_out)]

    rows_a = jnp.concatenate(my_heads(core), axis=1)
    rows_b = exchanged(jnp.concatenate(my_heads(1 - core), axis=1))

    spans = tokens // SPAN
    by_device = span_table.reshape(chips, 2, spans)
    mine = lax.dynamic_index_in_dim(by_device, core, 1, False)
    theirs = lax.dynamic_index_in_dim(by_device, 1 - core, 1, False)
    slot_pos = jnp.concatenate([mine.reshape(-1), theirs.reshape(-1)])
    chip = me // 2
    my_pos = jnp.concatenate(
        [
            lax.dynamic_index_in_dim(mine, chip, 0, False),
            lax.dynamic_index_in_dim(theirs, chip, 0, False),
        ]
    )

    by_span = (chips * spans, SPAN, keys_values.shape[1])
    dq_a, dq_b, dkv_a, dkv_b = attention_grads(
        slot_pos, my_pos, kv_a.reshape(by_span), kv_b.reshape(by_span), rows_a, rows_b
    )
    dkv = (dkv_a.astype(f32) + exchanged(dkv_b).astype(f32)).astype(bf16)
    terms = lax.all_to_all(
        dkv.reshape(chips, tokens, -1), "ctx", 0, 0, axis_index_groups=same_core
    )
    kv_grad = jnp.sum(terms.astype(f32), axis=0).astype(bf16)
    all_groups = lax.all_to_all(to_all(kv_grad, groups), "tp", 0, 0)
    input_grad = project(all_groups, weight)
    dq_other = exchanged(dq_b)
    query_grad = jnp.where(
        core == 0,
        jnp.concatenate([dq_a, dq_other], axis=1),
        jnp.concatenate([dq_other, dq_a], axis=1),
    )
    return query_grad, input_grad


def solution(mesh):
    placed = (P("ctx", "tp"), P("ctx", "tp"), P("ctx", "tp"), P("ctx", "tp"), P(None, "tp"), P())
    return jax.shard_map(
        on_device,
        mesh=mesh,
        in_specs=placed,
        out_specs=(P("ctx", "tp"), P("ctx", "tp")),
        check_vma=False,
    )
```

```python
import functools

import jax
import jax.numpy as jnp
from jax import lax
from jax.experimental import pallas as pl
from jax.experimental.pallas import tpu as pltpu
from jax.sharding import PartitionSpec as P

HEAD = 64
SPAN = 64
BLOCK = 512
PAIR = 2 * HEAD
SCALE = 0.125
LOG2E = 1.4426950408889634
MASKED = -1e30

f32 = jnp.float32
bf16 = jnp.bfloat16


def dot_t(a, b):
    return lax.dot_general(a, b, (((1,), (1,)), ((), ())), preferred_element_type=f32)


def dot(a, b):
    return lax.dot_general(a, b, (((1,), (0,)), ((), ())), preferred_element_type=f32)


def swap_halves(x):
    return pltpu.roll(x.astype(f32), HEAD, 1)


def prepare_kernel(rows_a, rows_b, mixed, plain):
    spans = rows_a.shape[0] // SPAN
    width = rows_a.shape[1] // 3
    pairs = width // PAIR
    qcount = pairs * SPAN
    line = lax.broadcasted_iota(jnp.int32, (HEAD, qcount), 0)

    def parts(d):
        a = d.astype(bf16).astype(f32)
        b = (d - a).astype(bf16).astype(f32)
        c = d - a - b
        return jnp.where(line == 0, a, jnp.where(line == 1, b, jnp.where(line == 2, c, 0.0)))

    for which, rows in enumerate((rows_a, rows_b)):
        for i in range(spans):
            n = which * spans + i

            def turned(part):
                stack = jnp.concatenate(
                    [
                        rows[i * SPAN : (i + 1) * SPAN, part * width + p * PAIR : part * width + (p + 1) * PAIR]
                        for p in range(pairs)
                    ],
                    axis=0,
                )
                return jnp.transpose(stack.astype(f32))

            q = turned(0)
            do = turned(1)
            prod = do * turned(2)
            q2 = q * (SCALE * LOG2E)
            hi = q2.astype(bf16).astype(f32)
            lo = q2 - hi
            for e in range(2):
                part = slice(e * HEAD, (e + 1) * HEAD)
                cols = slice(e * qcount, (e + 1) * qcount)
                mixed[n, 0, 0:HEAD, cols] = hi[part].astype(bf16)
                mixed[n, 0, HEAD:PAIR, cols] = lo[part].astype(bf16)
                mixed[n, 1, 0:HEAD, cols] = do[part].astype(bf16)
                mixed[n, 1, HEAD:PAIR, cols] = parts(-jnp.sum(prod[part], axis=0, keepdims=True)).astype(bf16)
                plain[n, :, cols] = q[part].astype(bf16)


def prepared_rows(rows_a, rows_b):
    spans = 2 * rows_a.shape[0] // SPAN
    qcount = rows_a.shape[1] // 3 // PAIR * SPAN
    vmem = pl.BlockSpec(memory_space=pltpu.VMEM)
    return pl.pallas_call(
        prepare_kernel,
        out_shape=(
            jax.ShapeDtypeStruct((spans, 2, PAIR, 2 * qcount), bf16),
            jax.ShapeDtypeStruct((spans, HEAD, 2 * qcount), bf16),
        ),
        in_specs=[vmem, vmem],
        out_specs=(vmem, vmem),
        compiler_params=pltpu.CompilerParams(vmem_limit_bytes=16 * 1024 * 1024),
        cost_estimate=pl.CostEstimate(flops=1 << 24, bytes_accessed=3 << 20, transcendentals=0),
    )(rows_a, rows_b)


def attention_kernel(
    slot_pos,
    my_pos,
    kv_a,
    kv_b,
    mixed,
    plain,
    dq,
    dkv_a,
    dkv_b,
    kv_sorted,
    kk,
    va,
    kt,
    scores_0,
    scores_1,
    weights_0,
    weights_1,
    dscores_0,
    dscores_1,
    acc,
    dqt,
):
    scores = (scores_0, scores_1)
    weights = (weights_0, weights_1)
    dscores = (dscores_0, dscores_1)
    half_slots = kv_a.shape[0]
    blocks = kk.shape[0]
    per_block = BLOCK // SPAN
    qcount = plain.shape[2] // 2
    pairs = qcount // SPAN

    def place(slot, _):
        for which, src in enumerate((kv_a, kv_b)):
            p = slot_pos[which * half_slots + slot]
            row = pl.multiple_of((p % per_block) * SPAN, SPAN)
            kv_sorted[p // per_block, pl.ds(row, SPAN), :] = src[slot]
        return 0

    lax.fori_loop(0, half_slots, place, 0, unroll=8)

    lane_k = lax.broadcasted_iota(jnp.int32, (BLOCK, PAIR), 1)
    low_k = lane_k < HEAD
    ones_hi = ((lane_k >= HEAD) & (lane_k < HEAD + 3)).astype(f32)

    def prepare(b, _):
        kv = kv_sorted[b].astype(f32)
        vk = pltpu.roll(kv, HEAD, 1)
        kk[b] = jnp.where(low_k, kv, vk).astype(bf16)
        va[b] = jnp.where(low_k, vk, ones_hi).astype(bf16)
        kt[b] = jnp.transpose(kv)[:HEAD].astype(bf16)
        acc[b] = jnp.zeros((PAIR, BLOCK), f32)
        return 0

    lax.fori_loop(0, blocks, prepare, 0)

    key_row = lax.broadcasted_iota(jnp.int32, (BLOCK, 2 * qcount), 0)
    query_row = lax.broadcasted_iota(jnp.int32, (BLOCK, 2 * qcount), 1) % SPAN

    def one_span(n, _):
        pos = my_pos[n]
        last = pos // per_block

        def block_of(u):
            return jnp.where(u == 0, last, u - 1)

        def products(u, parity, masked=False):
            s = dot(kk[block_of(u)], mixed[n, 0])
            if masked:
                s = jnp.where(key_row <= (pos % per_block) * SPAN + query_row, s, MASKED)
            scores[parity][u // 2] = s
            return jnp.max(s, axis=0, keepdims=True)

        def summed(u, parity, top):
            return jnp.sum(jnp.exp2(scores[parity][u // 2] - top), axis=0, keepdims=True)

        def stats(u, parity, running):
            top, l = running
            higher = jnp.maximum(top, products(u, parity))
            l = l + summed(u - 1, 1 - parity, top)
            return higher, l * jnp.exp2(top - higher)

        def terms(u, parity):
            p = jnp.exp2(scores[parity][u // 2] - lse)
            ds = p * dot(va[block_of(u)], mixed[n, 1])
            weights[parity][...] = p.astype(bf16)
            dscores[parity][...] = ds.astype(bf16)

        def sums(u, parity):
            b = block_of(u)
            ds = dscores[parity][...]
            dqt[...] += dot(kt[b], ds)
            acc[b, 0:HEAD] += dot_t(plain[n], ds)
            acc[b, HEAD:PAIR] += dot_t(mixed[n, 1, 0:HEAD], weights[parity][...])

        def both(t, running):
            running = stats(2 * t + 1, 1, running)
            return stats(2 * t + 2, 0, running)

        pairs_left = last // 2
        odd = last % 2 == 1
        running = (products(0, 0, True), jnp.zeros((1, 2 * qcount), f32))
        running = lax.fori_loop(0, pairs_left, both, running)

        def with_odd(running):
            top, l = stats(last, 1, running)
            return top, l + summed(last, 1, top)

        def without(running):
            top, l = running
            return top, l + summed(last, 0, top)

        top, l = lax.cond(odd, with_odd, without, running)
        lse = top + jnp.log2(l)

        dqt[...] = jnp.zeros_like(dqt)
        terms(0, 0)

        def grads(t, _):
            sums(2 * t, 0)
            terms(2 * t + 1, 1)
            sums(2 * t + 1, 1)
            terms(2 * t + 2, 0)
            return 0

        lax.fori_loop(0, pairs_left, grads, 0)

        @pl.when(odd)
        def _():
            sums(last - 1, 0)
            terms(last, 1)
            sums(last, 1)

        @pl.when(jnp.logical_not(odd))
        def _():
            sums(last, 0)

        total = jnp.concatenate([dqt[:, :qcount], dqt[:, qcount:]], axis=0)
        total = (jnp.transpose(total) * SCALE).astype(bf16)
        row = pl.multiple_of(n * SPAN, SPAN)
        for p in range(pairs):
            dq[pl.ds(row, SPAN), p * PAIR : (p + 1) * PAIR] = total[p * SPAN : (p + 1) * SPAN]
        return 0

    lax.fori_loop(0, plain.shape[0], one_span, 0)

    line = lax.broadcasted_iota(jnp.int32, (PAIR, BLOCK), 0)
    factor = jnp.where(line < HEAD, SCALE, 1.0)

    def finish(b, _):
        kv_sorted[b] = jnp.transpose(acc[b] * factor).astype(bf16)
        return 0

    lax.fori_loop(0, blocks, finish, 0)

    def collect(slot, _):
        for which, dst in enumerate((dkv_a, dkv_b)):
            p = slot_pos[which * half_slots + slot]
            row = pl.multiple_of((p % per_block) * SPAN, SPAN)
            dst[slot] = kv_sorted[p // per_block, pl.ds(row, SPAN), :]
        return 0

    lax.fori_loop(0, half_slots, collect, 0, unroll=8)


def attention_grads(slot_pos, my_pos, kv_a, kv_b, prepared):
    mixed, plain = prepared
    slots = 2 * kv_a.shape[0]
    blocks = slots * SPAN // BLOCK
    half_blocks = (blocks + 1) // 2
    spans = plain.shape[0]
    qcount = plain.shape[2] // 2
    pairs = qcount // SPAN
    smem = pl.BlockSpec(memory_space=pltpu.SMEM)
    vmem = pl.BlockSpec(memory_space=pltpu.VMEM)
    terms = slots * SPAN * spans * qcount * 2
    return pl.pallas_call(
        attention_kernel,
        out_shape=(
            jax.ShapeDtypeStruct((spans * SPAN, pairs * PAIR), bf16),
            jax.ShapeDtypeStruct(kv_a.shape, bf16),
            jax.ShapeDtypeStruct(kv_b.shape, bf16),
        ),
        in_specs=[smem, smem, vmem, vmem, vmem, vmem],
        out_specs=(vmem, vmem, vmem),
        scratch_shapes=[
            pltpu.VMEM((blocks, BLOCK, PAIR), bf16),
            pltpu.VMEM((blocks, BLOCK, PAIR), bf16),
            pltpu.VMEM((blocks, BLOCK, PAIR), bf16),
            pltpu.VMEM((blocks, HEAD, BLOCK), bf16),
            pltpu.VMEM((half_blocks, BLOCK, 2 * qcount), f32),
            pltpu.VMEM((half_blocks, BLOCK, 2 * qcount), f32),
            pltpu.VMEM((BLOCK, 2 * qcount), bf16),
            pltpu.VMEM((BLOCK, 2 * qcount), bf16),
            pltpu.VMEM((BLOCK, 2 * qcount), bf16),
            pltpu.VMEM((BLOCK, 2 * qcount), bf16),
            pltpu.VMEM((blocks, PAIR, BLOCK), f32),
            pltpu.VMEM((HEAD, 2 * qcount), f32),
        ],
        compiler_params=pltpu.CompilerParams(vmem_limit_bytes=48 * 1024 * 1024),
        cost_estimate=pl.CostEstimate(flops=terms * HEAD * 2 * 5 * 4, bytes_accessed=6 << 20, transcendentals=terms),
    )(slot_pos, my_pos, kv_a, kv_b, mixed, plain)


def project_kernel(core, kv, w_mine, w_other, out):
    rows = w_mine.shape[1]
    for w, part in ((w_mine, core[0]), (w_other, 1 - core[0])):
        total = dot_t(w[0], kv[0])
        for g in range(1, kv.shape[0]):
            total = total + dot_t(w[g], kv[g])
        out[pl.ds(pl.multiple_of(part * rows, 16), rows), :] = total.astype(bf16)


def project(core, kv, w_mine, w_other):
    smem = pl.BlockSpec(memory_space=pltpu.SMEM)
    vmem = pl.BlockSpec(memory_space=pltpu.VMEM)
    return pl.pallas_call(
        project_kernel,
        out_shape=jax.ShapeDtypeStruct((2 * w_mine.shape[1], kv.shape[1]), bf16),
        in_specs=[smem, vmem, vmem, vmem],
        out_specs=vmem,
        compiler_params=pltpu.CompilerParams(vmem_limit_bytes=24 * 1024 * 1024),
        cost_estimate=pl.CostEstimate(
            flops=4 * kv.size * w_mine.shape[1], bytes_accessed=4 * w_mine.size, transcendentals=0
        ),
    )(core[None], kv, w_mine, w_other).T


def on_device(queries, keys_values, forward_out, out_grad, kv_weight, span_table):
    tokens = queries.shape[0]
    half = queries.shape[1] // 2
    me = lax.axis_index("ctx")
    core = me % 2
    chip = me // 2
    count = lax.axis_size("ctx")
    groups = lax.axis_size("tp")
    chips = count // 2
    same_core = [[2 * c + k for c in range(chips)] for k in range(2)]
    other_core = [(i, i ^ 1) for i in range(count)]

    def to_all(x, n):
        return jnp.broadcast_to(x[None], (n,) + x.shape)

    def exchanged(x):
        return lax.ppermute(x, "ctx", other_core)

    kv_a = lax.all_to_all(to_all(keys_values, chips), "ctx", 0, 0, axis_index_groups=same_core)

    features = kv_weight.shape[0] // groups
    w_part = lax.dynamic_index_in_dim(
        kv_weight.reshape(groups, 2, features // 2, kv_weight.shape[1]), core, 1, False
    )
    kv_a, w_part = lax.optimization_barrier((kv_a, w_part))
    w_mine = lax.all_to_all(w_part, "tp", 0, 0)
    kv_b = exchanged(kv_a)

    def my_heads(k):
        return [lax.dynamic_slice_in_dim(x, k * half, half, 1) for x in (queries, out_grad, forward_out)]

    rows_a = jnp.concatenate(my_heads(core), axis=1)
    rows_b = exchanged(jnp.concatenate(my_heads(1 - core), axis=1))

    spans = tokens // SPAN
    by_device = span_table.reshape(chips, 2, spans)
    mine = lax.dynamic_index_in_dim(by_device, core, 1, False)
    theirs = lax.dynamic_index_in_dim(by_device, 1 - core, 1, False)
    slot_pos = jnp.concatenate([mine.reshape(-1), theirs.reshape(-1)])
    my_pos = jnp.concatenate(
        [
            lax.dynamic_index_in_dim(mine, chip, 0, False),
            lax.dynamic_index_in_dim(theirs, chip, 0, False),
        ]
    )

    by_span = (chips * spans, SPAN, keys_values.shape[1])
    prepared = prepared_rows(rows_a, rows_b)
    dq, dkv_a, dkv_b = attention_grads(
        slot_pos, my_pos, kv_a.reshape(by_span), kv_b.reshape(by_span), prepared
    )
    dkv_b, w_mine = lax.optimization_barrier((dkv_b, w_mine))
    dkv = (dkv_a.astype(f32) + exchanged(dkv_b).astype(f32)).astype(bf16)
    w_other = exchanged(w_mine)
    terms = lax.all_to_all(
        dkv.reshape(chips, tokens, -1), "ctx", 0, 0, axis_index_groups=same_core
    )
    kv_grad = jnp.sum(terms.astype(f32), axis=0).astype(bf16)
    all_groups = lax.all_to_all(to_all(kv_grad, groups), "tp", 0, 0)
    input_grad = project(core, all_groups, w_mine, w_other)
    dq_a = dq[:tokens]
    dq_b = exchanged(dq[tokens:])
    query_grad = jnp.where(
        core == 0,
        jnp.concatenate([dq_a, dq_b], axis=1),
        jnp.concatenate([dq_b, dq_a], axis=1),
    )
    return query_grad, input_grad


def solution(mesh):
    placed = (P("ctx", "tp"), P("ctx", "tp"), P("ctx", "tp"), P("ctx", "tp"), P(None, "tp"), P())
    return jax.shard_map(
        on_device,
        mesh=mesh,
        in_specs=placed,
        out_specs=(P("ctx", "tp"), P("ctx", "tp")),
        check_vma=False,
    )
```

```python
import functools

import jax
import jax.numpy as jnp
from jax import lax
from jax.experimental import pallas as pl
from jax.experimental.pallas import tpu as pltpu
from jax.sharding import PartitionSpec as P

HEAD = 64
SPAN = 64
BLOCK = 512
PAIR = 2 * HEAD
SCALE = 0.125
LOG2E = 1.4426950408889634
MASKED = -1e30

f32 = jnp.float32
bf16 = jnp.bfloat16


def dot_t(a, b):
    return lax.dot_general(a, b, (((1,), (1,)), ((), ())), preferred_element_type=f32)


def dot(a, b):
    return lax.dot_general(a, b, (((1,), (0,)), ((), ())), preferred_element_type=f32)


def swap_halves(x):
    return pltpu.roll(x.astype(f32), HEAD, 1)


def prepare_kernel(rows_a, rows_b, mixed, plain):
    spans = rows_a.shape[0] // SPAN
    width = rows_a.shape[1] // 3
    pairs = width // PAIR
    qcount = pairs * SPAN
    line = lax.broadcasted_iota(jnp.int32, (HEAD, qcount), 0)

    def parts(d):
        a = d.astype(bf16).astype(f32)
        b = (d - a).astype(bf16).astype(f32)
        c = d - a - b
        return jnp.where(line == 0, a, jnp.where(line == 1, b, jnp.where(line == 2, c, 0.0)))

    for which, rows in enumerate((rows_a, rows_b)):
        for i in range(spans):
            n = which * spans + i

            def turned(part):
                stack = jnp.concatenate(
                    [
                        rows[i * SPAN : (i + 1) * SPAN, part * width + p * PAIR : part * width + (p + 1) * PAIR]
                        for p in range(pairs)
                    ],
                    axis=0,
                )
                return jnp.transpose(stack.astype(f32))

            q = turned(0)
            do = turned(1)
            prod = do * turned(2)
            q2 = q * (SCALE * LOG2E)
            hi = q2.astype(bf16).astype(f32)
            lo = q2 - hi
            for e in range(2):
                part = slice(e * HEAD, (e + 1) * HEAD)
                cols = slice(e * qcount, (e + 1) * qcount)
                mixed[n, 0, 0:HEAD, cols] = hi[part].astype(bf16)
                mixed[n, 0, HEAD:PAIR, cols] = lo[part].astype(bf16)
                mixed[n, 1, 0:HEAD, cols] = do[part].astype(bf16)
                mixed[n, 1, HEAD:PAIR, cols] = parts(-jnp.sum(prod[part], axis=0, keepdims=True)).astype(bf16)
                plain[n, :, cols] = q[part].astype(bf16)


def prepared_rows(rows_a, rows_b):
    spans = 2 * rows_a.shape[0] // SPAN
    qcount = rows_a.shape[1] // 3 // PAIR * SPAN
    vmem = pl.BlockSpec(memory_space=pltpu.VMEM)
    return pl.pallas_call(
        prepare_kernel,
        out_shape=(
            jax.ShapeDtypeStruct((spans, 2, PAIR, 2 * qcount), bf16),
            jax.ShapeDtypeStruct((spans, HEAD, 2 * qcount), bf16),
        ),
        in_specs=[vmem, vmem],
        out_specs=(vmem, vmem),
        compiler_params=pltpu.CompilerParams(vmem_limit_bytes=8 * 1024 * 1024),
        cost_estimate=pl.CostEstimate(flops=1 << 24, bytes_accessed=3 << 20, transcendentals=0),
    )(rows_a, rows_b)


def attention_kernel(
    slot_pos,
    my_pos,
    kv_a,
    kv_b,
    mixed,
    plain,
    dq,
    dkv_a,
    dkv_b,
    kv_sorted,
    kk,
    va,
    kt,
    scores_0,
    scores_1,
    held_0,
    held_1,
    dscores_0,
    dscores_1,
    tops,
    acc,
    dqt,
):
    scores = (scores_0, scores_1)
    held = (held_0, held_1)
    dscores = (dscores_0, dscores_1)
    half_slots = kv_a.shape[0]
    blocks = kk.shape[0]
    per_block = BLOCK // SPAN
    qcount = plain.shape[2] // 2
    pairs = qcount // SPAN

    def place(slot, _):
        for which, src in enumerate((kv_a, kv_b)):
            p = slot_pos[which * half_slots + slot]
            row = pl.multiple_of((p % per_block) * SPAN, SPAN)
            kv_sorted[p // per_block, pl.ds(row, SPAN), :] = src[slot]
        return 0

    lax.fori_loop(0, half_slots, place, 0, unroll=8)

    lane_k = lax.broadcasted_iota(jnp.int32, (BLOCK, PAIR), 1)
    low_k = lane_k < HEAD
    ones_hi = ((lane_k >= HEAD) & (lane_k < HEAD + 3)).astype(f32)

    def prepare(b, _):
        kv = kv_sorted[b].astype(f32)
        vk = pltpu.roll(kv, HEAD, 1)
        kk[b] = jnp.where(low_k, kv, vk).astype(bf16)
        va[b] = jnp.where(low_k, vk, ones_hi).astype(bf16)
        kt[b] = jnp.transpose(kv)[:HEAD].astype(bf16)
        acc[b] = jnp.zeros((PAIR, BLOCK), f32)
        return 0

    lax.fori_loop(0, blocks, prepare, 0, unroll=4)

    key_row = lax.broadcasted_iota(jnp.int32, (BLOCK, 2 * qcount), 0)
    query_row = lax.broadcasted_iota(jnp.int32, (BLOCK, 2 * qcount), 1) % SPAN

    def one_span(n, _):
        pos = my_pos[n]
        last = pos // per_block

        def block_of(u):
            return jnp.where(u == 0, last, u - 1)

        def first(u, parity, top, masked=False):
            s = dot(kk[block_of(u)], mixed[n, 0])
            if masked:
                s = jnp.where(key_row <= (pos % per_block) * SPAN + query_row, s, MASKED)
            scores[parity][...] = s
            return jnp.maximum(top, jnp.max(s, axis=0, keepdims=True))

        def second(u, parity, top, before, l):
            p = jnp.exp2(scores[parity][...] - top)
            ds = p * dot(va[block_of(u)], mixed[n, 1])
            ds = ds.astype(bf16)
            dscores[parity][...] = ds
            held[parity][u // 2, 0] = jnp.transpose(ds)
            held[parity][u // 2, 1] = jnp.transpose(p.astype(bf16))
            tops[u] = top
            return l * jnp.exp2(before - top) + jnp.sum(p, axis=0, keepdims=True)

        def third(u, parity, top, before):
            dqt[...] = dqt[...] * jnp.exp2(before - top) + dot(kt[block_of(u)], dscores[parity][...])

        def step(u, parity, carry):
            top, before, earlier, l = carry
            l = second(u - 1, 1 - parity, top, before, l)
            higher = first(u, parity, top)
            third(u - 2, parity, before, earlier)
            return higher, top, before, l

        dqt[...] = jnp.zeros_like(dqt)
        lowest = jnp.full((1, 2 * qcount), MASKED, f32)
        nothing = jnp.zeros((1, 2 * qcount), f32)
        start = first(0, 0, lowest, True)

        def alone(_):
            l = second(0, 0, start, lowest, nothing)
            third(0, 0, start, lowest)
            return start, l

        def several(_):
            l = second(0, 0, start, lowest, nothing)
            carry = (first(1, 1, start), start, lowest, l)

            def two(t, carry):
                return step(2 * t + 3, 1, step(2 * t + 2, 0, carry))

            carry = lax.fori_loop(0, (last - 1) // 2, two, carry)

            def tail(parity, carry):
                top, before, earlier, l = carry
                third(last - 1, 1 - parity, before, earlier)
                l = second(last, parity, top, before, l)
                third(last, parity, top, before)
                return top, l

            return lax.cond(
                last % 2 == 0, lambda c: tail(0, step(last, 0, c)), lambda c: tail(1, c), carry
            )

        top, l = lax.cond(last == 0, alone, several, 0)
        lse = top + jnp.log2(l)
        share = jnp.exp2(top - lse)

        def summed(u, parity):
            f = jnp.exp2(tops[u] - lse)
            dk = dot((plain[n].astype(f32) * f).astype(bf16), held[parity][u // 2, 0])
            dv = dot((mixed[n, 1, 0:HEAD].astype(f32) * f).astype(bf16), held[parity][u // 2, 1])
            return jnp.concatenate([dk, dv], axis=0)

        def sums_two(t, _):
            even = summed(2 * t, 0)
            odd = summed(2 * t + 1, 1)
            acc[block_of(2 * t)] += even
            acc[block_of(2 * t + 1)] += odd
            return 0

        lax.fori_loop(0, (last + 1) // 2, sums_two, 0)

        @pl.when(last % 2 == 0)
        def _():
            acc[block_of(last)] += summed(last, 0)

        dqt[...] = dqt[...] * share
        total = jnp.concatenate([dqt[:, :qcount], dqt[:, qcount:]], axis=0)
        total = (jnp.transpose(total) * SCALE).astype(bf16)
        row = pl.multiple_of(n * SPAN, SPAN)
        for p in range(pairs):
            dq[pl.ds(row, SPAN), p * PAIR : (p + 1) * PAIR] = total[p * SPAN : (p + 1) * SPAN]
        return 0

    lax.fori_loop(0, plain.shape[0], one_span, 0)

    line = lax.broadcasted_iota(jnp.int32, (PAIR, BLOCK), 0)
    factor = jnp.where(line < HEAD, SCALE, 1.0)

    def finish(b, _):
        kv_sorted[b] = jnp.transpose(acc[b] * factor).astype(bf16)
        return 0

    lax.fori_loop(0, blocks, finish, 0, unroll=4)

    def collect(slot, _):
        for which, dst in enumerate((dkv_a, dkv_b)):
            p = slot_pos[which * half_slots + slot]
            row = pl.multiple_of((p % per_block) * SPAN, SPAN)
            dst[slot] = kv_sorted[p // per_block, pl.ds(row, SPAN), :]
        return 0

    lax.fori_loop(0, half_slots, collect, 0, unroll=8)


def attention_grads(slot_pos, my_pos, kv_a, kv_b, prepared):
    mixed, plain = prepared
    slots = 2 * kv_a.shape[0]
    blocks = slots * SPAN // BLOCK
    half_blocks = (blocks + 1) // 2
    spans = plain.shape[0]
    qcount = plain.shape[2] // 2
    pairs = qcount // SPAN
    smem = pl.BlockSpec(memory_space=pltpu.SMEM)
    vmem = pl.BlockSpec(memory_space=pltpu.VMEM)
    terms = slots * SPAN * spans * qcount * 2
    return pl.pallas_call(
        attention_kernel,
        out_shape=(
            jax.ShapeDtypeStruct((spans * SPAN, pairs * PAIR), bf16),
            jax.ShapeDtypeStruct(kv_a.shape, bf16),
            jax.ShapeDtypeStruct(kv_b.shape, bf16),
        ),
        in_specs=[smem, smem, vmem, vmem, vmem, vmem],
        out_specs=(vmem, vmem, vmem),
        scratch_shapes=[
            pltpu.VMEM((blocks, BLOCK, PAIR), bf16),
            pltpu.VMEM((blocks, BLOCK, PAIR), bf16),
            pltpu.VMEM((blocks, BLOCK, PAIR), bf16),
            pltpu.VMEM((blocks, HEAD, BLOCK), bf16),
            pltpu.VMEM((BLOCK, 2 * qcount), f32),
            pltpu.VMEM((BLOCK, 2 * qcount), f32),
            pltpu.VMEM((half_blocks, 2, 2 * qcount, BLOCK), bf16),
            pltpu.VMEM((half_blocks, 2, 2 * qcount, BLOCK), bf16),
            pltpu.VMEM((BLOCK, 2 * qcount), bf16),
            pltpu.VMEM((BLOCK, 2 * qcount), bf16),
            pltpu.VMEM((blocks, 1, 2 * qcount), f32),
            pltpu.VMEM((blocks, PAIR, BLOCK), f32),
            pltpu.VMEM((HEAD, 2 * qcount), f32),
        ],
        compiler_params=pltpu.CompilerParams(vmem_limit_bytes=26 * 1024 * 1024),
        cost_estimate=pl.CostEstimate(flops=1 << 20, bytes_accessed=1 << 16, transcendentals=0),
    )(slot_pos, my_pos, kv_a, kv_b, mixed, plain)


def project_kernel(core, kv, w_mine, w_other, out):
    rows = w_mine.shape[1]
    for w, part in ((w_mine, core[0]), (w_other, 1 - core[0])):
        total = None
        for g in range(0, kv.shape[0], 2):
            term = dot_t(
                jnp.concatenate([w[g], w[g + 1]], axis=1), jnp.concatenate([kv[g], kv[g + 1]], axis=1)
            )
            total = term if total is None else total + term
        out[pl.ds(pl.multiple_of(part * rows, 16), rows), :] = total.astype(bf16)


def project(core, kv, w_mine, w_other):
    smem = pl.BlockSpec(memory_space=pltpu.SMEM)
    vmem = pl.BlockSpec(memory_space=pltpu.VMEM)
    return pl.pallas_call(
        project_kernel,
        out_shape=jax.ShapeDtypeStruct((2 * w_mine.shape[1], kv.shape[1]), bf16),
        in_specs=[smem, vmem, vmem, vmem],
        out_specs=vmem,
        compiler_params=pltpu.CompilerParams(vmem_limit_bytes=12 * 1024 * 1024),
        cost_estimate=pl.CostEstimate(
            flops=4 * kv.size * w_mine.shape[1], bytes_accessed=4 * w_mine.size, transcendentals=0
        ),
    )(core[None], kv, w_mine, w_other).T


def on_device(queries, keys_values, forward_out, out_grad, kv_weight, span_table):
    tokens = queries.shape[0]
    half = queries.shape[1] // 2
    me = lax.axis_index("ctx")
    core = me % 2
    chip = me // 2
    count = lax.axis_size("ctx")
    groups = lax.axis_size("tp")
    chips = count // 2
    same_core = [[2 * c + k for c in range(chips)] for k in range(2)]
    other_core = [(i, i ^ 1) for i in range(count)]

    def to_all(x, n):
        return jnp.broadcast_to(x[None], (n,) + x.shape)

    def exchanged(x):
        return lax.ppermute(x, "ctx", other_core)

    kv_a = lax.all_to_all(to_all(keys_values, chips), "ctx", 0, 0, axis_index_groups=same_core)

    features = kv_weight.shape[0] // groups
    w_part = lax.dynamic_index_in_dim(
        kv_weight.reshape(groups, 2, features // 2, kv_weight.shape[1]), core, 1, False
    )
    kv_a, w_part = lax.optimization_barrier((kv_a, w_part))
    w_mine = lax.all_to_all(w_part, "tp", 0, 0)
    kv_b = exchanged(kv_a)

    def my_heads(k):
        return [lax.dynamic_slice_in_dim(x, k * half, half, 1) for x in (queries, out_grad, forward_out)]

    rows_a = jnp.concatenate(my_heads(core), axis=1)
    rows_b = exchanged(jnp.concatenate(my_heads(1 - core), axis=1))

    spans = tokens // SPAN
    by_device = span_table.reshape(chips, 2, spans)
    mine = lax.dynamic_index_in_dim(by_device, core, 1, False)
    theirs = lax.dynamic_index_in_dim(by_device, 1 - core, 1, False)
    slot_pos = jnp.concatenate([mine.reshape(-1), theirs.reshape(-1)])
    my_pos = jnp.concatenate(
        [
            lax.dynamic_index_in_dim(mine, chip, 0, False),
            lax.dynamic_index_in_dim(theirs, chip, 0, False),
        ]
    )

    by_span = (chips * spans, SPAN, keys_values.shape[1])
    prepared = prepared_rows(rows_a, rows_b)
    dq, dkv_a, dkv_b = attention_grads(
        slot_pos, my_pos, kv_a.reshape(by_span), kv_b.reshape(by_span), prepared
    )
    dkv_a, w_mine = lax.optimization_barrier((dkv_a, w_mine))
    dkv = (dkv_a.astype(f32) + exchanged(dkv_b).astype(f32)).astype(bf16)
    w_other = exchanged(w_mine)
    terms = lax.all_to_all(
        dkv.reshape(chips, tokens, -1), "ctx", 0, 0, axis_index_groups=same_core
    )
    kv_grad = jnp.sum(terms.astype(f32), axis=0).astype(bf16)
    all_groups = lax.all_to_all(to_all(kv_grad, groups), "tp", 0, 0)
    input_grad = project(core, all_groups, w_mine, w_other)
    dq_a = dq[:tokens]
    dq_b = exchanged(dq[tokens:])
    query_grad = jnp.where(
        core == 0,
        jnp.concatenate([dq_a, dq_b], axis=1),
        jnp.concatenate([dq_b, dq_a], axis=1),
    )
    return query_grad, input_grad


def solution(mesh):
    placed = (P("ctx", "tp"), P("ctx", "tp"), P("ctx", "tp"), P("ctx", "tp"), P(None, "tp"), P())
    return jax.shard_map(
        on_device,
        mesh=mesh,
        in_specs=placed,
        out_specs=(P("ctx", "tp"), P("ctx", "tp")),
        check_vma=False,
    )
```

```python
import functools

import jax
import jax.numpy as jnp
from jax import lax
from jax.experimental import pallas as pl
from jax.experimental.pallas import tpu as pltpu
from jax.sharding import PartitionSpec as P

HEAD = 64
SPAN = 64
BLOCK = 512
PAIR = 2 * HEAD
SCALE = 0.125
LOG2E = 1.4426950408889634
MASKED = -1e30

f32 = jnp.float32
bf16 = jnp.bfloat16


def dot_t(a, b):
    return lax.dot_general(a, b, (((1,), (1,)), ((), ())), preferred_element_type=f32)


def dot(a, b):
    return lax.dot_general(a, b, (((1,), (0,)), ((), ())), preferred_element_type=f32)


def swap_halves(x):
    return pltpu.roll(x.astype(f32), HEAD, 1)


def prepare_kernel(rows_a, rows_b, mixed, plain):
    spans = rows_a.shape[0] // SPAN
    width = rows_a.shape[1] // 3
    pairs = width // PAIR
    qcount = pairs * SPAN
    line = lax.broadcasted_iota(jnp.int32, (HEAD, qcount), 0)

    def parts(d):
        a = d.astype(bf16).astype(f32)
        b = (d - a).astype(bf16).astype(f32)
        c = d - a - b
        return jnp.where(line == 0, a, jnp.where(line == 1, b, jnp.where(line == 2, c, 0.0)))

    for which, rows in enumerate((rows_a, rows_b)):
        for i in range(spans):
            n = which * spans + i

            def turned(part):
                stack = jnp.concatenate(
                    [
                        rows[i * SPAN : (i + 1) * SPAN, part * width + p * PAIR : part * width + (p + 1) * PAIR]
                        for p in range(pairs)
                    ],
                    axis=0,
                )
                return jnp.transpose(stack.astype(f32))

            q = turned(0)
            do = turned(1)
            prod = do * turned(2)
            q2 = q * (SCALE * LOG2E)
            hi = q2.astype(bf16).astype(f32)
            lo = q2 - hi
            for e in range(2):
                part = slice(e * HEAD, (e + 1) * HEAD)
                cols = slice(e * qcount, (e + 1) * qcount)
                mixed[n, 0, 0:HEAD, cols] = hi[part].astype(bf16)
                mixed[n, 0, HEAD:PAIR, cols] = lo[part].astype(bf16)
                mixed[n, 1, 0:HEAD, cols] = do[part].astype(bf16)
                mixed[n, 1, HEAD:PAIR, cols] = parts(-jnp.sum(prod[part], axis=0, keepdims=True)).astype(bf16)
                plain[n, :, cols] = q[part].astype(bf16)


def prepared_rows(rows_a, rows_b):
    spans = 2 * rows_a.shape[0] // SPAN
    qcount = rows_a.shape[1] // 3 // PAIR * SPAN
    vmem = pl.BlockSpec(memory_space=pltpu.VMEM)
    return pl.pallas_call(
        prepare_kernel,
        out_shape=(
            jax.ShapeDtypeStruct((spans, 2, PAIR, 2 * qcount), bf16),
            jax.ShapeDtypeStruct((spans, HEAD, 2 * qcount), bf16),
        ),
        in_specs=[vmem, vmem],
        out_specs=(vmem, vmem),
        compiler_params=pltpu.CompilerParams(vmem_limit_bytes=8 * 1024 * 1024),
        cost_estimate=pl.CostEstimate(flops=1 << 24, bytes_accessed=3 << 20, transcendentals=0),
    )(rows_a, rows_b)


def attention_kernel(
    slot_pos,
    my_pos,
    kv_a,
    kv_b,
    mixed,
    plain,
    dq,
    dkv_a,
    dkv_b,
    kv_sorted,
    kk,
    va,
    kt,
    scores_0,
    scores_1,
    held_0,
    held_1,
    dscores_0,
    dscores_1,
    tops,
    acc,
    dqt,
):
    scores = (scores_0, scores_1)
    held = (held_0, held_1)
    dscores = (dscores_0, dscores_1)
    half_slots = kv_a.shape[0]
    blocks = kk.shape[0]
    per_block = BLOCK // SPAN
    qcount = plain.shape[2] // 2
    pairs = qcount // SPAN

    def place(slot, _):
        for which, src in enumerate((kv_a, kv_b)):
            p = slot_pos[which * half_slots + slot]
            row = pl.multiple_of((p % per_block) * SPAN, SPAN)
            kv_sorted[p // per_block, pl.ds(row, SPAN), :] = src[slot]
        return 0

    lax.fori_loop(0, half_slots, place, 0, unroll=8)

    lane_k = lax.broadcasted_iota(jnp.int32, (BLOCK, PAIR), 1)
    low_k = lane_k < HEAD
    ones_hi = ((lane_k >= HEAD) & (lane_k < HEAD + 3)).astype(f32)

    def prepare(b, _):
        kv = kv_sorted[b].astype(f32)
        vk = pltpu.roll(kv, HEAD, 1)
        kk[b] = jnp.where(low_k, kv, vk).astype(bf16)
        va[b] = jnp.where(low_k, vk, ones_hi).astype(bf16)
        kt[b] = jnp.transpose(kv)[:HEAD].astype(bf16)
        acc[b] = jnp.zeros((PAIR, BLOCK), f32)
        return 0

    lax.fori_loop(0, blocks, prepare, 0, unroll=4)

    key_row = lax.broadcasted_iota(jnp.int32, (BLOCK, 2 * qcount), 0)
    query_row = lax.broadcasted_iota(jnp.int32, (BLOCK, 2 * qcount), 1) % SPAN

    def one_span(n, _):
        pos = my_pos[n]
        last = pos // per_block

        def block_of(u):
            return jnp.where(u == 0, last, u - 1)

        def first(u, parity, top, masked=False):
            s = dot(kk[block_of(u)], mixed[n, 0])
            if masked:
                s = jnp.where(key_row <= (pos % per_block) * SPAN + query_row, s, MASKED)
            scores[parity][...] = s
            return jnp.maximum(top, jnp.max(s, axis=0, keepdims=True))

        def second(u, parity, top, before, l):
            p = jnp.exp2(scores[parity][...] - top)
            ds = p * dot(va[block_of(u)], mixed[n, 1])
            ds = ds.astype(bf16)
            dscores[parity][...] = ds
            held[parity][u // 2, 0] = jnp.transpose(ds)
            held[parity][u // 2, 1] = jnp.transpose(p.astype(bf16))
            tops[u] = top
            return l * jnp.exp2(before - top) + jnp.sum(p, axis=0, keepdims=True)

        def third(u, parity, top, before):
            dqt[...] = dqt[...] * jnp.exp2(before - top) + dot(kt[block_of(u)], dscores[parity][...])

        def step(u, parity, carry):
            top, before, earlier, l = carry
            l = second(u - 1, 1 - parity, top, before, l)
            higher = first(u, parity, top)
            third(u - 2, parity, before, earlier)
            return higher, top, before, l

        dqt[...] = jnp.zeros_like(dqt)
        lowest = jnp.full((1, 2 * qcount), MASKED, f32)
        nothing = jnp.zeros((1, 2 * qcount), f32)
        start = first(0, 0, lowest, True)

        def alone(_):
            l = second(0, 0, start, lowest, nothing)
            third(0, 0, start, lowest)
            return start, l

        def several(_):
            l = second(0, 0, start, lowest, nothing)
            carry = (first(1, 1, start), start, lowest, l)

            def two(t, carry):
                return step(2 * t + 3, 1, step(2 * t + 2, 0, carry))

            carry = lax.fori_loop(0, (last - 1) // 2, two, carry)

            def tail(parity, carry):
                top, before, earlier, l = carry
                third(last - 1, 1 - parity, before, earlier)
                l = second(last, parity, top, before, l)
                third(last, parity, top, before)
                return top, l

            return lax.cond(
                last % 2 == 0, lambda c: tail(0, step(last, 0, c)), lambda c: tail(1, c), carry
            )

        top, l = lax.cond(last == 0, alone, several, 0)
        lse = top + jnp.log2(l)
        share = jnp.exp2(top - lse)

        def summed(u, parity):
            f = jnp.exp2(tops[u] - lse)
            dk = dot((plain[n].astype(f32) * f).astype(bf16), held[parity][u // 2, 0])
            dv = dot((mixed[n, 1, 0:HEAD].astype(f32) * f).astype(bf16), held[parity][u // 2, 1])
            return jnp.concatenate([dk, dv], axis=0)

        def sums_two(t, _):
            even = summed(2 * t, 0)
            odd = summed(2 * t + 1, 1)
            acc[block_of(2 * t)] += even
            acc[block_of(2 * t + 1)] += odd
            return 0

        lax.fori_loop(0, (last + 1) // 2, sums_two, 0)

        @pl.when(last % 2 == 0)
        def _():
            acc[block_of(last)] += summed(last, 0)

        dqt[...] = dqt[...] * share
        total = jnp.concatenate([dqt[:, :qcount], dqt[:, qcount:]], axis=0)
        total = (jnp.transpose(total) * SCALE).astype(bf16)
        row = pl.multiple_of(n * SPAN, SPAN)
        for p in range(pairs):
            dq[pl.ds(row, SPAN), p * PAIR : (p + 1) * PAIR] = total[p * SPAN : (p + 1) * SPAN]
        return 0

    lax.fori_loop(0, plain.shape[0], one_span, 0)

    line = lax.broadcasted_iota(jnp.int32, (PAIR, BLOCK), 0)
    factor = jnp.where(line < HEAD, SCALE, 1.0)

    def finish(b, _):
        kv_sorted[b] = jnp.transpose(acc[b] * factor).astype(bf16)
        return 0

    lax.fori_loop(0, blocks, finish, 0, unroll=4)

    def collect(slot, _):
        for which, dst in enumerate((dkv_a, dkv_b)):
            p = slot_pos[which * half_slots + slot]
            row = pl.multiple_of((p % per_block) * SPAN, SPAN)
            dst[slot] = kv_sorted[p // per_block, pl.ds(row, SPAN), :]
        return 0

    lax.fori_loop(0, half_slots, collect, 0, unroll=8)


def attention_grads(slot_pos, my_pos, kv_a, kv_b, prepared):
    mixed, plain = prepared
    slots = 2 * kv_a.shape[0]
    blocks = slots * SPAN // BLOCK
    half_blocks = (blocks + 1) // 2
    spans = plain.shape[0]
    qcount = plain.shape[2] // 2
    pairs = qcount // SPAN
    smem = pl.BlockSpec(memory_space=pltpu.SMEM)
    vmem = pl.BlockSpec(memory_space=pltpu.VMEM)
    terms = slots * SPAN * spans * qcount * 2
    return pl.pallas_call(
        attention_kernel,
        out_shape=(
            jax.ShapeDtypeStruct((spans * SPAN, pairs * PAIR), bf16),
            jax.ShapeDtypeStruct(kv_a.shape, bf16),
            jax.ShapeDtypeStruct(kv_b.shape, bf16),
        ),
        in_specs=[smem, smem, vmem, vmem, vmem, vmem],
        out_specs=(vmem, vmem, vmem),
        scratch_shapes=[
            pltpu.VMEM((blocks, BLOCK, PAIR), bf16),
            pltpu.VMEM((blocks, BLOCK, PAIR), bf16),
            pltpu.VMEM((blocks, BLOCK, PAIR), bf16),
            pltpu.VMEM((blocks, HEAD, BLOCK), bf16),
            pltpu.VMEM((BLOCK, 2 * qcount), f32),
            pltpu.VMEM((BLOCK, 2 * qcount), f32),
            pltpu.VMEM((half_blocks, 2, 2 * qcount, BLOCK), bf16),
            pltpu.VMEM((half_blocks, 2, 2 * qcount, BLOCK), bf16),
            pltpu.VMEM((BLOCK, 2 * qcount), bf16),
            pltpu.VMEM((BLOCK, 2 * qcount), bf16),
            pltpu.VMEM((blocks, 1, 2 * qcount), f32),
            pltpu.VMEM((blocks, PAIR, BLOCK), f32),
            pltpu.VMEM((HEAD, 2 * qcount), f32),
        ],
        compiler_params=pltpu.CompilerParams(vmem_limit_bytes=20 * 1024 * 1024),
        cost_estimate=pl.CostEstimate(flops=1 << 20, bytes_accessed=1 << 16, transcendentals=0),
    )(slot_pos, my_pos, kv_a, kv_b, mixed, plain)


def project_kernel(core, kv, w_mine, w_other, out):
    rows = w_mine.shape[1]
    for w, part in ((w_mine, core[0]), (w_other, 1 - core[0])):
        total = None
        for g in range(0, kv.shape[0], 2):
            term = dot_t(
                jnp.concatenate([w[g], w[g + 1]], axis=1), jnp.concatenate([kv[g], kv[g + 1]], axis=1)
            )
            total = term if total is None else total + term
        out[pl.ds(pl.multiple_of(part * rows, 16), rows), :] = total.astype(bf16)


def project(core, kv, w_mine, w_other):
    smem = pl.BlockSpec(memory_space=pltpu.SMEM)
    vmem = pl.BlockSpec(memory_space=pltpu.VMEM)
    return pl.pallas_call(
        project_kernel,
        out_shape=jax.ShapeDtypeStruct((2 * w_mine.shape[1], kv.shape[1]), bf16),
        in_specs=[smem, vmem, vmem, vmem],
        out_specs=vmem,
        compiler_params=pltpu.CompilerParams(vmem_limit_bytes=12 * 1024 * 1024),
        cost_estimate=pl.CostEstimate(
            flops=4 * kv.size * w_mine.shape[1], bytes_accessed=4 * w_mine.size, transcendentals=0
        ),
    )(core[None], kv, w_mine, w_other).T


def on_device(queries, keys_values, forward_out, out_grad, kv_weight, span_table):
    tokens = queries.shape[0]
    half = queries.shape[1] // 2
    me = lax.axis_index("ctx")
    core = me % 2
    chip = me // 2
    count = lax.axis_size("ctx")
    groups = lax.axis_size("tp")
    chips = count // 2
    same_core = [[2 * c + k for c in range(chips)] for k in range(2)]
    other_core = [(i, i ^ 1) for i in range(count)]

    def to_all(x, n):
        return jnp.broadcast_to(x[None], (n,) + x.shape)

    def exchanged(x):
        return lax.ppermute(x, "ctx", other_core)

    kv_a = lax.all_to_all(to_all(keys_values, chips), "ctx", 0, 0, axis_index_groups=same_core)

    features = kv_weight.shape[0] // groups
    w_part = lax.dynamic_index_in_dim(
        kv_weight.reshape(groups, 2, features // 2, kv_weight.shape[1]), core, 1, False
    )

    def my_heads(k):
        return [lax.dynamic_slice_in_dim(x, k * half, half, 1) for x in (queries, out_grad, forward_out)]

    rows_a = jnp.concatenate(my_heads(core), axis=1)
    rows_b = exchanged(jnp.concatenate(my_heads(1 - core), axis=1))

    kv_a, w_part, rows_b = lax.optimization_barrier((kv_a, w_part, rows_b))
    w_mine = lax.all_to_all(w_part, "tp", 0, 0)
    kv_b = exchanged(kv_a)

    spans = tokens // SPAN
    by_device = span_table.reshape(chips, 2, spans)
    mine = lax.dynamic_index_in_dim(by_device, core, 1, False)
    theirs = lax.dynamic_index_in_dim(by_device, 1 - core, 1, False)
    slot_pos = jnp.concatenate([mine.reshape(-1), theirs.reshape(-1)])
    my_pos = jnp.concatenate(
        [
            lax.dynamic_index_in_dim(mine, chip, 0, False),
            lax.dynamic_index_in_dim(theirs, chip, 0, False),
        ]
    )

    by_span = (chips * spans, SPAN, keys_values.shape[1])
    prepared = prepared_rows(rows_a, rows_b)
    dq, dkv_a, dkv_b = attention_grads(
        slot_pos, my_pos, kv_a.reshape(by_span), kv_b.reshape(by_span), prepared
    )
    dkv_a, w_mine = lax.optimization_barrier((dkv_a, w_mine))
    dkv = (dkv_a.astype(f32) + exchanged(dkv_b).astype(f32)).astype(bf16)
    w_other = exchanged(w_mine)
    terms = lax.all_to_all(
        dkv.reshape(chips, tokens, -1), "ctx", 0, 0, axis_index_groups=same_core
    )
    kv_grad = jnp.sum(terms.astype(f32), axis=0).astype(bf16)
    all_groups = lax.all_to_all(to_all(kv_grad, groups), "tp", 0, 0)
    input_grad = project(core, all_groups, w_mine, w_other)
    dq_a = dq[:tokens]
    dq_b = exchanged(dq[tokens:])
    query_grad = jnp.where(
        core == 0,
        jnp.concatenate([dq_a, dq_b], axis=1),
        jnp.concatenate([dq_b, dq_a], axis=1),
    )
    return query_grad, input_grad


def solution(mesh):
    placed = (P("ctx", "tp"), P("ctx", "tp"), P("ctx", "tp"), P("ctx", "tp"), P(None, "tp"), P())
    return jax.shard_map(
        on_device,
        mesh=mesh,
        in_specs=placed,
        out_specs=(P("ctx", "tp"), P("ctx", "tp")),
        check_vma=False,
    )
```

```python
import functools

import jax
import jax.numpy as jnp
from jax import lax
from jax.experimental import pallas as pl
from jax.experimental.pallas import tpu as pltpu
from jax.sharding import PartitionSpec as P

HEAD = 64
SPAN = 64
BLOCK = 512
AT_ONCE = 4
PAIR = 2 * HEAD
SCALE = 0.125
LOG2E = 1.4426950408889634
MASKED = -1e30

f32 = jnp.float32
bf16 = jnp.bfloat16


def dot_t(a, b):
    return lax.dot_general(a, b, (((1,), (1,)), ((), ())), preferred_element_type=f32)


def dot(a, b):
    return lax.dot_general(a, b, (((1,), (0,)), ((), ())), preferred_element_type=f32)


def swap_halves(x):
    return pltpu.roll(x.astype(f32), HEAD, 1)


def prepare_kernel(rows_a, rows_b, mixed, plain):
    spans = rows_a.shape[0] // SPAN
    width = rows_a.shape[1] // 3
    pairs = width // PAIR
    qcount = pairs * SPAN
    line = lax.broadcasted_iota(jnp.int32, (HEAD, qcount), 0)

    def parts(d):
        a = d.astype(bf16).astype(f32)
        b = (d - a).astype(bf16).astype(f32)
        c = d - a - b
        return jnp.where(line == 0, a, jnp.where(line == 1, b, jnp.where(line == 2, c, 0.0)))

    for which, rows in enumerate((rows_a, rows_b)):
        for i in range(spans):
            n = which * spans + i

            def turned(part):
                stack = jnp.concatenate(
                    [
                        rows[i * SPAN : (i + 1) * SPAN, part * width + p * PAIR : part * width + (p + 1) * PAIR]
                        for p in range(pairs)
                    ],
                    axis=0,
                )
                return jnp.transpose(stack.astype(f32))

            q = turned(0)
            do = turned(1)
            prod = do * turned(2)
            q2 = q * (SCALE * LOG2E)
            hi = q2.astype(bf16).astype(f32)
            lo = q2 - hi
            for e in range(2):
                part = slice(e * HEAD, (e + 1) * HEAD)
                cols = slice(e * qcount, (e + 1) * qcount)
                mixed[n, 0, 0:HEAD, cols] = hi[part].astype(bf16)
                mixed[n, 0, HEAD:PAIR, cols] = lo[part].astype(bf16)
                mixed[n, 1, 0:HEAD, cols] = do[part].astype(bf16)
                mixed[n, 1, HEAD:PAIR, cols] = parts(-jnp.sum(prod[part], axis=0, keepdims=True)).astype(bf16)
                plain[n, :, cols] = q[part].astype(bf16)


def prepared_rows(rows_a, rows_b):
    spans = 2 * rows_a.shape[0] // SPAN
    qcount = rows_a.shape[1] // 3 // PAIR * SPAN
    vmem = pl.BlockSpec(memory_space=pltpu.VMEM)
    return pl.pallas_call(
        prepare_kernel,
        out_shape=(
            jax.ShapeDtypeStruct((spans, 2, PAIR, 2 * qcount), bf16),
            jax.ShapeDtypeStruct((spans, HEAD, 2 * qcount), bf16),
        ),
        in_specs=[vmem, vmem],
        out_specs=(vmem, vmem),
        compiler_params=pltpu.CompilerParams(vmem_limit_bytes=8 * 1024 * 1024),
        cost_estimate=pl.CostEstimate(flops=1 << 24, bytes_accessed=3 << 20, transcendentals=0),
    )(rows_a, rows_b)


def attention_kernel(
    slot_pos,
    my_pos,
    kv_a,
    kv_b,
    mixed,
    plain,
    dq,
    dkv_a,
    dkv_b,
    kv_sorted,
    kk,
    va,
    kt,
    scores_0,
    scores_1,
    held,
    dscores_0,
    dscores_1,
    tops,
    lses,
    acc,
    dqt,
):
    scores = (scores_0, scores_1)
    dscores = (dscores_0, dscores_1)
    half_slots = kv_a.shape[0]
    blocks = kk.shape[0]
    per_block = BLOCK // SPAN
    qcount = plain.shape[2] // 2
    pairs = qcount // SPAN

    def place(slot, _):
        for which, src in enumerate((kv_a, kv_b)):
            p = slot_pos[which * half_slots + slot]
            row = pl.multiple_of((p % per_block) * SPAN, SPAN)
            kv_sorted[p // per_block, pl.ds(row, SPAN), :] = src[slot]
        return 0

    lax.fori_loop(0, half_slots, place, 0, unroll=8)

    lane_k = lax.broadcasted_iota(jnp.int32, (BLOCK, PAIR), 1)
    low_k = lane_k < HEAD
    ones_hi = ((lane_k >= HEAD) & (lane_k < HEAD + 3)).astype(f32)

    def prepare(b, _):
        kv = kv_sorted[b].astype(f32)
        vk = pltpu.roll(kv, HEAD, 1)
        kk[b] = jnp.where(low_k, kv, vk).astype(bf16)
        va[b] = jnp.where(low_k, vk, ones_hi).astype(bf16)
        kt[b] = jnp.transpose(kv)[:HEAD].astype(bf16)
        acc[b] = jnp.zeros((PAIR, BLOCK), f32)
        return 0

    lax.fori_loop(0, blocks, prepare, 0, unroll=4)

    key_row = lax.broadcasted_iota(jnp.int32, (BLOCK, 2 * qcount), 0)
    query_row = lax.broadcasted_iota(jnp.int32, (BLOCK, 2 * qcount), 1) % SPAN

    def one_span(n, _):
        pos = my_pos[n]
        last = pos // per_block

        def block_of(u):
            return jnp.where(u == 0, last, u - 1)

        def first(u, parity, top, masked=False):
            s = dot(kk[block_of(u)], mixed[n, 0])
            if masked:
                s = jnp.where(key_row <= (pos % per_block) * SPAN + query_row, s, MASKED)
            scores[parity][...] = s
            return jnp.maximum(top, jnp.max(s, axis=0, keepdims=True))

        def second(u, parity, top, before, l):
            p = jnp.exp2(scores[parity][...] - top)
            ds = p * dot(va[block_of(u)], mixed[n, 1])
            ds = ds.astype(bf16)
            dscores[parity][...] = ds
            held[n, u, 0] = jnp.transpose(ds)
            held[n, u, 1] = jnp.transpose(p.astype(bf16))
            tops[n, u] = top
            return l * jnp.exp2(before - top) + jnp.sum(p, axis=0, keepdims=True)

        def third(u, parity, top, before):
            dqt[...] = dqt[...] * jnp.exp2(before - top) + dot(kt[block_of(u)], dscores[parity][...])

        def step(u, parity, carry):
            top, before, earlier, l = carry
            l = second(u - 1, 1 - parity, top, before, l)
            higher = first(u, parity, top)
            third(u - 2, parity, before, earlier)
            return higher, top, before, l

        dqt[...] = jnp.zeros_like(dqt)
        lowest = jnp.full((1, 2 * qcount), MASKED, f32)
        nothing = jnp.zeros((1, 2 * qcount), f32)
        start = first(0, 0, lowest, True)

        def alone(_):
            l = second(0, 0, start, lowest, nothing)
            third(0, 0, start, lowest)
            return start, l

        def several(_):
            l = second(0, 0, start, lowest, nothing)
            carry = (first(1, 1, start), start, lowest, l)

            def two(t, carry):
                return step(2 * t + 3, 1, step(2 * t + 2, 0, carry))

            carry = lax.fori_loop(0, (last - 1) // 2, two, carry)

            def tail(parity, carry):
                top, before, earlier, l = carry
                third(last - 1, 1 - parity, before, earlier)
                l = second(last, parity, top, before, l)
                third(last, parity, top, before)
                return top, l

            return lax.cond(
                last % 2 == 0, lambda c: tail(0, step(last, 0, c)), lambda c: tail(1, c), carry
            )

        top, l = lax.cond(last == 0, alone, several, 0)
        lses[n] = top + jnp.log2(l)
        dqt[...] = dqt[...] * jnp.exp2(top - lses[n])
        total = jnp.concatenate([dqt[:, :qcount], dqt[:, qcount:]], axis=0)
        total = (jnp.transpose(total) * SCALE).astype(bf16)
        row = pl.multiple_of(n * SPAN, SPAN)
        for p in range(pairs):
            dq[pl.ds(row, SPAN), p * PAIR : (p + 1) * PAIR] = total[p * SPAN : (p + 1) * SPAN]
        return 0

    lax.fori_loop(0, plain.shape[0], one_span, 0)

    spans = mixed.shape[0]
    lasts = [my_pos[n] // per_block for n in range(spans)]
    ends = [lasts[0] + 1]
    for n in range(1, spans):
        ends.append(ends[-1] + lasts[n] + 1)

    def located(i):
        n, u, last = 0, i, lasts[0]
        for k in range(1, spans):
            later = i >= ends[k - 1]
            n = jnp.where(later, k, n)
            u = jnp.where(later, i - ends[k - 1], u)
            last = jnp.where(later, lasts[k], last)
        return n, u, jnp.where(u == 0, last, u - 1)

    def summed(n, u):
        f = jnp.exp2(tops[n, u] - lses[n])
        dk = dot((plain[n].astype(f32) * f).astype(bf16), held[n, u, 0])
        dv = dot((mixed[n, 1, 0:HEAD].astype(f32) * f).astype(bf16), held[n, u, 1])
        return jnp.concatenate([dk, dv], axis=0)

    def sums_several(first, count):
        places = [located(first + k) for k in range(count)]
        results = [summed(n, u) for n, u, _ in places]
        for (_, _, b), result in zip(places, results):
            acc[b] += result

    def sums_step(t, _):
        sums_several(t * AT_ONCE, AT_ONCE)
        return 0

    def sums_rest(i, _):
        sums_several(i, 1)
        return 0

    rounds = ends[-1] // AT_ONCE
    lax.fori_loop(0, rounds, sums_step, 0)
    lax.fori_loop(rounds * AT_ONCE, ends[-1], sums_rest, 0)

    line = lax.broadcasted_iota(jnp.int32, (PAIR, BLOCK), 0)
    factor = jnp.where(line < HEAD, SCALE, 1.0)

    def finish(b, _):
        kv_sorted[b] = jnp.transpose(acc[b] * factor).astype(bf16)
        return 0

    lax.fori_loop(0, blocks, finish, 0, unroll=4)

    def collect(slot, _):
        for which, dst in enumerate((dkv_a, dkv_b)):
            p = slot_pos[which * half_slots + slot]
            row = pl.multiple_of((p % per_block) * SPAN, SPAN)
            dst[slot] = kv_sorted[p // per_block, pl.ds(row, SPAN), :]
        return 0

    lax.fori_loop(0, half_slots, collect, 0, unroll=8)


def attention_grads(slot_pos, my_pos, kv_a, kv_b, prepared):
    mixed, plain = prepared
    slots = 2 * kv_a.shape[0]
    blocks = slots * SPAN // BLOCK
    spans = plain.shape[0]
    qcount = plain.shape[2] // 2
    pairs = qcount // SPAN
    smem = pl.BlockSpec(memory_space=pltpu.SMEM)
    vmem = pl.BlockSpec(memory_space=pltpu.VMEM)
    terms = slots * SPAN * spans * qcount * 2
    return pl.pallas_call(
        attention_kernel,
        out_shape=(
            jax.ShapeDtypeStruct((spans * SPAN, pairs * PAIR), bf16),
            jax.ShapeDtypeStruct(kv_a.shape, bf16),
            jax.ShapeDtypeStruct(kv_b.shape, bf16),
        ),
        in_specs=[smem, smem, vmem, vmem, vmem, vmem],
        out_specs=(vmem, vmem, vmem),
        scratch_shapes=[
            pltpu.VMEM((blocks, BLOCK, PAIR), bf16),
            pltpu.VMEM((blocks, BLOCK, PAIR), bf16),
            pltpu.VMEM((blocks, BLOCK, PAIR), bf16),
            pltpu.VMEM((blocks, HEAD, BLOCK), bf16),
            pltpu.VMEM((BLOCK, 2 * qcount), f32),
            pltpu.VMEM((BLOCK, 2 * qcount), f32),
            pltpu.VMEM((spans, blocks, 2, 2 * qcount, BLOCK), bf16),
            pltpu.VMEM((BLOCK, 2 * qcount), bf16),
            pltpu.VMEM((BLOCK, 2 * qcount), bf16),
            pltpu.VMEM((spans, blocks, 1, 2 * qcount), f32),
            pltpu.VMEM((spans, 1, 2 * qcount), f32),
            pltpu.VMEM((blocks, PAIR, BLOCK), f32),
            pltpu.VMEM((HEAD, 2 * qcount), f32),
        ],
        compiler_params=pltpu.CompilerParams(vmem_limit_bytes=45 * 1024 * 1024),
        cost_estimate=pl.CostEstimate(flops=1 << 20, bytes_accessed=1 << 16, transcendentals=0),
    )(slot_pos, my_pos, kv_a, kv_b, mixed, plain)


def project_kernel(core, kv, w_mine, w_other, out):
    rows = w_mine.shape[1]
    for w, part in ((w_mine, core[0]), (w_other, 1 - core[0])):
        total = None
        for g in range(0, kv.shape[0], 2):
            term = dot_t(
                jnp.concatenate([w[g], w[g + 1]], axis=1), jnp.concatenate([kv[g], kv[g + 1]], axis=1)
            )
            total = term if total is None else total + term
        out[pl.ds(pl.multiple_of(part * rows, 16), rows), :] = total.astype(bf16)


def project(core, kv, w_mine, w_other):
    smem = pl.BlockSpec(memory_space=pltpu.SMEM)
    vmem = pl.BlockSpec(memory_space=pltpu.VMEM)
    return pl.pallas_call(
        project_kernel,
        out_shape=jax.ShapeDtypeStruct((2 * w_mine.shape[1], kv.shape[1]), bf16),
        in_specs=[smem, vmem, vmem, vmem],
        out_specs=vmem,
        compiler_params=pltpu.CompilerParams(vmem_limit_bytes=12 * 1024 * 1024),
        cost_estimate=pl.CostEstimate(
            flops=4 * kv.size * w_mine.shape[1], bytes_accessed=4 * w_mine.size, transcendentals=0
        ),
    )(core[None], kv, w_mine, w_other).T


def on_device(queries, keys_values, forward_out, out_grad, kv_weight, span_table):
    tokens = queries.shape[0]
    half = queries.shape[1] // 2
    me = lax.axis_index("ctx")
    core = me % 2
    chip = me // 2
    count = lax.axis_size("ctx")
    groups = lax.axis_size("tp")
    chips = count // 2
    same_core = [[2 * c + k for c in range(chips)] for k in range(2)]
    other_core = [(i, i ^ 1) for i in range(count)]

    def to_all(x, n):
        return jnp.broadcast_to(x[None], (n,) + x.shape)

    def exchanged(x):
        return lax.ppermute(x, "ctx", other_core)

    kv_a = lax.all_to_all(to_all(keys_values, chips), "ctx", 0, 0, axis_index_groups=same_core)

    features = kv_weight.shape[0] // groups
    w_part = lax.dynamic_index_in_dim(
        kv_weight.reshape(groups, 2, features // 2, kv_weight.shape[1]), core, 1, False
    )

    def my_heads(k):
        return [lax.dynamic_slice_in_dim(x, k * half, half, 1) for x in (queries, out_grad, forward_out)]

    rows_a = jnp.concatenate(my_heads(core), axis=1)
    rows_b = exchanged(jnp.concatenate(my_heads(1 - core), axis=1))

    kv_a, w_part, rows_b = lax.optimization_barrier((kv_a, w_part, rows_b))
    w_mine = lax.all_to_all(w_part, "tp", 0, 0)
    kv_b = exchanged(kv_a)

    spans = tokens // SPAN
    by_device = span_table.reshape(chips, 2, spans)
    mine = lax.dynamic_index_in_dim(by_device, core, 1, False)
    theirs = lax.dynamic_index_in_dim(by_device, 1 - core, 1, False)
    slot_pos = jnp.concatenate([mine.reshape(-1), theirs.reshape(-1)])
    my_pos = jnp.concatenate(
        [
            lax.dynamic_index_in_dim(mine, chip, 0, False),
            lax.dynamic_index_in_dim(theirs, chip, 0, False),
        ]
    )

    by_span = (chips * spans, SPAN, keys_values.shape[1])
    prepared = prepared_rows(rows_a, rows_b)
    dq, dkv_a, dkv_b = attention_grads(
        slot_pos, my_pos, kv_a.reshape(by_span), kv_b.reshape(by_span), prepared
    )
    dkv_a, w_mine = lax.optimization_barrier((dkv_a, w_mine))
    dkv = (dkv_a.astype(f32) + exchanged(dkv_b).astype(f32)).astype(bf16)
    w_other = exchanged(w_mine)
    terms = lax.all_to_all(
        dkv.reshape(chips, tokens, -1), "ctx", 0, 0, axis_index_groups=same_core
    )
    kv_grad = jnp.sum(terms.astype(f32), axis=0).astype(bf16)
    all_groups = lax.all_to_all(to_all(kv_grad, groups), "tp", 0, 0)
    input_grad = project(core, all_groups, w_mine, w_other)
    dq_a = dq[:tokens]
    dq_b = exchanged(dq[tokens:])
    query_grad = jnp.where(
        core == 0,
        jnp.concatenate([dq_a, dq_b], axis=1),
        jnp.concatenate([dq_b, dq_a], axis=1),
    )
    return query_grad, input_grad


def solution(mesh):
    placed = (P("ctx", "tp"), P("ctx", "tp"), P("ctx", "tp"), P("ctx", "tp"), P(None, "tp"), P())
    return jax.shard_map(
        on_device,
        mesh=mesh,
        in_specs=placed,
        out_specs=(P("ctx", "tp"), P("ctx", "tp")),
        check_vma=False,
    )
```
